32 devices in a mesh: tm: 4 (over z), rows: 8 (over y, x, core).
Axes of the slice: x: 2, y: 2, z: 4, core: 2. Of those that a mesh axis runs over, the one named last changes fastest.
Arguments:
- frames: bfloat16 [2, 8, 1408, 2000], P(None, 'rows', 'tm'), may hold values from -6 to 6
- resets: int32 [2, 8, 1408], P(None, 'rows', 'tm'), may hold values from 0 to 1, as said below
- valid_frames: int32 [2, 8, 1408], P(None, 'rows', 'tm'), may hold values from 0 to 1, as said below
- weight_one: bfloat16 [2000, 2000], replicated, may hold values from -0.125 to 0.125
- gain_one: float32 [2000], replicated, may hold values from 0.02 to 1.3
- bias_one: float32 [2000], replicated, may hold values from -0.5 to 0.5
- decay_one: float32 [2000], replicated, may hold values from 0.3 to 1
- weight_two: bfloat16 [2000, 2000], replicated, may hold values from -0.125 to 0.125
- gain_two: float32 [2000], replicated, may hold values from 0.02 to 1.3
- bias_two: float32 [2000], replicated, may hold values from -0.5 to 0.5
- decay_two: float32 [2000], replicated, may hold values from 0.3 to 1
- out_grad: bfloat16 [2, 8, 1408, 2000], P(None, 'rows', 'tm'), may hold values from -6 to 6
Outputs:
- output: float32 [2, 8, 1408, 2000], P(None, 'rows', 'tm')
- input_grad: float32 [2, 8, 1408, 2000], P(None, 'rows', 'tm')
- grad_weight_one: float32 [2000, 2000], P('tm')
- grad_gain_one: float32 [2000], replicated
- grad_bias_one: float32 [2000], replicated
- grad_decay_one: float32 [2000], replicated
- grad_weight_two: float32 [2000, 2000], P('tm')
- grad_gain_two: float32 [2000], replicated
- grad_bias_two: float32 [2000], replicated
- grad_decay_two: float32 [2000], replicated
- rms_value: float32 [], replicated
The draws below stay inside these ranges and needn't reach their ends.
Inputs may be any that keep to these rules, and one draw needn't show every extreme that they name: `resets`: frame 0 of every row is 1. In each micro-batch, of every 4 aligned rows exactly one, drawn from the seed, has no 1 after frame 0. `valid_frames`: each row is valid on a prefix of 704 frames or more; the row without later segment starts is valid on all 1408 frames.
All inputs are finite; a program needn't handle non-finite values.
Results may differ from the reference program's by a relative error of at most 0.0038.
Values may be sent and summed in bfloat16 or wider, within the bound.
No kernel may reach another device: no remote copies, remote signals or barrier semaphores. Data moves between devices by JAX's collectives and lax.ppermute only.
A program may use at most 192 MiB of HBM per device.

```python
import jax
import jax.numpy as jnp
from jax import lax

H = 2000
SEQ = 1408
MICRO = 2
ROWS = 8


def long_rows(key):
    picked = jax.random.randint(key, (MICRO, ROWS // 4, 1), 0, 4)
    slots = jnp.arange(4)[None, None, :]
    return (slots == picked).reshape(MICRO, ROWS)


def draw_resets(key, part):
    longer = long_rows(key)
    key = jax.random.fold_in(key, 11)
    marks = jax.random.randint(key, (MICRO, ROWS, SEQ), 0, SEQ) < 4
    leading = jnp.arange(SEQ)[None, None, :] == 0
    flags = marks & jnp.logical_not(longer[:, :, None]) | leading
    return flags.astype(jnp.int32)


def draw_valid_frames(key, part):
    longer = long_rows(key)
    key = jax.random.fold_in(key, 23)
    lengths = jax.random.randint(key, (MICRO, ROWS, 1), SEQ // 2, SEQ + 1)
    lengths = jnp.where(longer[:, :, None], SEQ, lengths)
    return (jnp.arange(SEQ)[None, None, :] < lengths).astype(jnp.int32)


def slow_units(key, layer_tag, share):
    key = jax.random.fold_in(key, layer_tag)
    return jax.random.uniform(key, (H,), jnp.float32) < share


def decay_values(key, slow):
    level = jax.random.uniform(key, (H,), jnp.float32)
    slow_rate = 1.0 - 0.0005 * level
    fast_rate = 1.0 - 0.1 * jnp.exp(level * jnp.log(7.0))
    return jnp.where(slow, slow_rate, fast_rate)


def gain_values(key, slow, low_end, high_end):
    level = jax.random.uniform(key, (H,), jnp.float32)
    return jnp.where(slow, 0.02 + 0.04 * level, low_end + (high_end - low_end) * level)


def bias_values(key, slow):
    level = jax.random.uniform(key, (H,), jnp.float32) * 2.0 - 1.0
    return jnp.where(slow, 0.002 * level, 0.5 * level)


def draw_decay_one(key, part):
    share = 0.5
    slow = slow_units(key, 101, share)
    key = jax.random.fold_in(key, 31)
    return decay_values(key, slow)


def draw_gain_one(key, part):
    share, low_end, high_end = (0.5, 0.8, 1.2)
    slow = slow_units(key, 101, share)
    key = jax.random.fold_in(key, 32)
    return gain_values(key, slow, low_end, high_end)


def draw_bias_one(key, part):
    share = 0.5
    slow = slow_units(key, 101, share)
    key = jax.random.fold_in(key, 33)
    return bias_values(key, slow)


def draw_decay_two(key, part):
    share = 0.5
    slow = slow_units(key, 202, share)
    key = jax.random.fold_in(key, 41)
    return decay_values(key, slow)


def draw_gain_two(key, part):
    share, low_end, high_end = (0.5, 0.8, 1.2)
    slow = slow_units(key, 202, share)
    key = jax.random.fold_in(key, 42)
    return gain_values(key, slow, low_end, high_end)


def draw_bias_two(key, part):
    share = 0.5
    slow = slow_units(key, 202, share)
    key = jax.random.fold_in(key, 43)
    return bias_values(key, slow)


def level_of(rng, extent, split, low, high):
    factor_of, own = 1.0, jax.random.fold_in(rng, 6)
    for axis_at, shards_of in split:
        heights = jnp.exp(jax.random.uniform(jax.random.fold_in(own, axis_at), (shards_of,), jnp.float32, low / len(split), high / len(split)))
        factor_of = factor_of * jnp.repeat(heights, extent[axis_at] // shards_of).reshape([-1 if axis == axis_at else 1 for axis in range(len(extent))])
    return factor_of


def scatter_about(key, extent, width, limit, split=(), kind=jnp.bfloat16):
    factor_of = level_of(key, extent, split, -0.22, 0.18) if split else 1.0
    result = jax.random.normal(key, extent, jnp.float32) * width * factor_of
    return jnp.minimum(jnp.maximum(result, -limit), limit).astype(kind)


def setup_inputs(seed: int = 0) -> dict:
    keys = jax.random.split(jax.random.key(seed), 13)
    frames = scatter_about(keys[0], (MICRO, ROWS, SEQ, H), 1.0, 6.0, ((1, 8), (2, 4)))
    resets = draw_resets(jax.random.fold_in(keys[12], 71), 0)
    valid_frames = draw_valid_frames(jax.random.fold_in(keys[12], 71), 0)
    weight_one = scatter_about(keys[3], (H, H), H ** -0.5, 0.125)
    gain_one = draw_gain_one(jax.random.fold_in(keys[12], 71), 0)
    bias_one = draw_bias_one(jax.random.fold_in(keys[12], 71), 0)
    decay_one = draw_decay_one(jax.random.fold_in(keys[12], 71), 0)
    weight_two = scatter_about(keys[7], (H, H), H ** -0.5, 0.125)
    gain_two = draw_gain_two(jax.random.fold_in(keys[12], 71), 0)
    bias_two = draw_bias_two(jax.random.fold_in(keys[12], 71), 0)
    decay_two = draw_decay_two(jax.random.fold_in(keys[12], 71), 0)
    out_grad = scatter_about(keys[11], (MICRO, ROWS, SEQ, H), 1.0, 6.0, ((1, 8), (2, 4)))
    return dict(frames=frames, resets=resets, valid_frames=valid_frames, weight_one=weight_one, gain_one=gain_one, bias_one=bias_one, decay_one=decay_one, weight_two=weight_two, gain_two=gain_two, bias_two=bias_two, decay_two=decay_two, out_grad=out_grad)


EPSILON = 1e-05

@jax.custom_vjp
def low(v):
    return lax.optimization_barrier(v.astype(jnp.bfloat16)).astype(jnp.float32)

@jax.custom_vjp
def low_back(v):
    return v

def low_keep(v):
    return (low(v), None)

def low_pass(kept, grad):
    return (grad,)

def back_keep(v):
    return (v, None)

def back_low(kept, grad):
    return (low(grad),)
low.defvjp(low_keep, low_pass)
low_back.defvjp(back_keep, back_low)

def smooth(values):
    return jax.nn.softplus(values)

def recurrence(pre_all, keep_mask, decay_vec):
    pre_time = jnp.moveaxis(pre_all, 2, 0)
    keep_time = jnp.moveaxis(keep_mask, 2, 0)

    def advance(carried, pieces):
        current, keep_step = pieces
        updated = smooth(current + decay_vec * keep_step[..., None] * carried)
        return (updated, updated)
    initial = jnp.zeros(pre_time.shape[1:], jnp.float32)
    _, states = lax.scan(advance, initial, (pre_time, keep_time))
    return jnp.moveaxis(states, 0, 2)

def indrnn_layer(inputs, weight, gain_vec, bias_vec, decay_vec, keep_mask, valid_mask, counts):
    projected = low_back(jnp.einsum('mrsh,hk->mrsk', inputs, weight, precision=lax.Precision.HIGHEST))
    centre = lax.optimization_barrier(jnp.sum(valid_mask * projected, axis=(1, 2))) / counts[:, None]
    centred = projected - centre[:, None, None, :]
    variance = lax.optimization_barrier(jnp.sum(valid_mask * centred * centred, axis=(1, 2))) / counts[:, None]
    normed = centred * lax.rsqrt(variance + EPSILON)[:, None, None, :]
    return recurrence(gain_vec * normed + bias_vec, keep_mask, decay_vec)

def reference(frames, resets, valid_frames, weight_one, gain_one, bias_one, decay_one, weight_two, gain_two, bias_two, decay_two, out_grad):
    keep_mask = 1.0 - resets.astype(jnp.float32)
    valid_mask = valid_frames.astype(jnp.float32)[..., None]
    counts = lax.optimization_barrier(jnp.sum(valid_frames.astype(jnp.float32), axis=(1, 2)))

    def forward(inputs, w_first, g_first, b_first, u_first, w_second, g_second, b_second, u_second):
        hidden_one = indrnn_layer(inputs, w_first, g_first, b_first, u_first, keep_mask, valid_mask, counts)
        hidden_two = indrnn_layer(low(hidden_one), w_second, g_second, b_second, u_second, keep_mask, valid_mask, counts)
        return (inputs + hidden_two, hidden_two)
    as_float = [arr.astype(jnp.float32) for arr in (frames, weight_one, gain_one, bias_one, decay_one, weight_two, gain_two, bias_two, decay_two)]
    output, pullback, hidden_two = jax.vjp(forward, *as_float, has_aux=True)
    gradients = pullback(out_grad.astype(jnp.float32))
    rms_value = jnp.sqrt(jnp.sum(valid_mask * hidden_two * hidden_two) / (jnp.sum(counts) * H))
    return (output, gradients[0], gradients[1], gradients[2], gradients[3], gradients[4], gradients[5], gradients[6], gradients[7], gradients[8], rms_value)
```

```python
import functools
import math

import jax
import jax.numpy as jnp
from jax import lax
from jax.experimental import pallas as pl
from jax.experimental.pallas import tpu as pltpu
from jax.sharding import PartitionSpec as P

EPSILON = 1e-05
LANES = 128
SUBS = 8
GROUP = LANES * SUBS
ROWS16 = 16
SPLIT = 3
LOG2E = 1.4426950408889634
LN2 = 0.6931471805599453


def limit(mebibytes):
    return pltpu.CompilerParams(vmem_limit_bytes=mebibytes * 1024 * 1024)


def vmem():
    return pl.BlockSpec(memory_space=pltpu.VMEM)


def smem():
    return pl.BlockSpec(memory_space=pltpu.SMEM)


def anywhere():
    return pl.BlockSpec(memory_space=pl.ANY)


def held(array):
    return pltpu.with_memory_space_constraint(array, pltpu.VMEM)


def distant(array):
    return pltpu.with_memory_space_constraint(array, pltpu.HBM)


def after(value, *earlier):
    return lax.optimization_barrier((value,) + earlier)[0]


def cost(flops, moved, transcendentals=0):
    return pl.CostEstimate(flops=flops, bytes_accessed=moved, transcendentals=transcendentals)


def groups_of(width):
    return -(-width // GROUP)


def as_tiles(vectors):
    count, width = vectors.shape
    groups = groups_of(width)
    padded = jnp.pad(vectors, ((0, 0), (0, groups * GROUP - width)))
    return padded.reshape(count, groups, SUBS, LANES)


def swapped(value, axis, distance):
    count = lax.axis_size(axis)
    return lax.ppermute(value, axis, [(at, at ^ distance) for at in range(count)])


def shifted(value, axis, steps):
    count = lax.axis_size(axis)
    first, last = (max(0, -steps), min(count, count - steps))
    return lax.ppermute(value, axis, [(at, at + steps) for at in range(first, last)])


def tree_sum(values):
    values = list(values)
    while len(values) > 1:
        values = [
            values[at] + values[at + 1] if at + 1 < len(values) else values[at]
            for at in range(0, len(values), 2)
        ]
    return values[0]


def bits_of(axis):
    return [1 << bit for bit in range(lax.axis_size(axis).bit_length() - 1)]


def piece_size(frames, most):
    return max(step for step in range(1, most + 1) if frames % step == 0)


def stat_row(plane, m, micro, groups, tile):
    group, sub = divmod(tile, SUBS)
    return ((plane * micro + m) * groups + group) * SUBS + sub


def project_block(block, cols, x, w, valid_ref, z_ref, z_first, stat_ref, micro, width):
    count = x.shape[0]
    streams = valid_ref.shape[0]
    frames = count // streams
    counts = jnp.sum(valid_ref[...].astype(jnp.float32), axis=1, keepdims=True)
    groups = groups_of(width)
    per_group = GROUP // cols
    group = block // per_group
    first_sub = lax.rem(block, per_group) * (cols // LANES)
    z = jnp.dot(x, w, preferred_element_type=jnp.float32)
    lane = lax.broadcasted_iota(jnp.int32, (1, LANES), 1)
    frame = lax.broadcasted_iota(jnp.int32, (frames, LANES), 0).astype(jnp.float32)
    for q in range(-(-z.shape[1] // LANES)):
        inside = lane + (block * cols + q * LANES) < width
        wide = min(LANES, z.shape[1] - q * LANES)
        for m in range(micro):
            number, first, second, pivot = 0.0, 0.0, 0.0, None
            for r in range(m * streams // micro, (m + 1) * streams // micro):
                part = z[r * frames : (r + 1) * frames, q * LANES : q * LANES + wide]
                if wide < LANES:
                    part = jnp.concatenate(
                        [part, jnp.zeros((frames, LANES - wide), jnp.float32)], axis=1
                    )
                part = jnp.where(inside, part, 0.0)
                pivot = part[0:1, :] if pivot is None else pivot
                valid = jnp.broadcast_to(counts[r : r + 1, :], (1, LANES))
                away = jnp.where(frame < valid, part - pivot, 0.0)
                number += valid
                first += jnp.sum(away, axis=0, keepdims=True)
                second += jnp.sum(away * away, axis=0, keepdims=True)
                at = (z_first + r * frames) * SUBS + first_sub + q
                z_ref[pl.ds(at, frames, stride=SUBS), :] = part
            spread = jnp.maximum(second - first * first / jnp.maximum(number, 1.0), 0.0)
            for plane, row in enumerate((first + number * pivot, spread, number)):
                at = ((plane * micro + m) * groups + group) * SUBS + first_sub + q
                stat_ref[pl.ds(at, 1), :] = row


def project_rows_kernel(micro, cols, valid_ref, x_hbm, w_hbm, z_ref, stat_ref, x_ref, w_ref, sems):
    count = x_ref.shape[0]
    width = w_ref.shape[1]
    groups = groups_of(width)
    blocks = [slice(at, min(width, at + cols)) for at in range(0, width, cols)]
    loads = [
        pltpu.make_async_copy(w_hbm.at[:, at], w_ref.at[:, at], sems.at[1 + n])
        for n, at in enumerate(blocks)
    ]
    load_x = pltpu.make_async_copy(x_hbm, x_ref, sems.at[0])
    load_x.start()
    loads[0].start()
    stat_ref[...] = jnp.zeros_like(stat_ref)
    load_x.wait()
    span = count // micro
    for tile in range(-(-width // LANES)):
        lanes = slice(tile * LANES, min(width, (tile + 1) * LANES))
        wide = lanes.stop - lanes.start
        for m in range(micro):
            part = x_ref[m * span : (m + 1) * span, lanes].astype(jnp.float32)
            at = stat_row(3, m, micro, groups, tile)
            stat_ref[at : at + 1, :wide] = jnp.sum(part, axis=0, keepdims=True)
    for block, at in enumerate(blocks):
        loads[block].wait()
        if block + 1 < len(blocks):
            loads[block + 1].start()
        group = block * cols // GROUP
        project_block(
            block, cols, x_ref[...], w_ref[:, at], valid_ref, z_ref, group * count, stat_ref, micro, width
        )


def project_tiles_kernel(micro, cols, valid_ref, s_ref, w_ref, z_ref, stat_ref, x_ref):
    count, depth = x_ref.shape
    width = w_ref.shape[1]
    groups = groups_of(width)
    span = count // micro
    stat_ref[...] = jnp.zeros_like(stat_ref)
    for tile in range(groups * SUBS):
        group, sub = divmod(tile, SUBS)
        wide = max(0, min(LANES, depth - tile * LANES))
        for m in range(micro):
            first = (group * count + m * span) * SUBS + sub
            if wide == 0:
                continue
            part = s_ref[pl.ds(first, span, stride=SUBS), :]
            at = stat_row(3, m, micro, groups, tile)
            stat_ref[at : at + 1, :wide] = jnp.sum(part, axis=0, keepdims=True)[:, :wide]
            x_ref[m * span : (m + 1) * span, tile * LANES : tile * LANES + wide] = part.astype(
                jnp.bfloat16
            )[:, :wide]
    for block in range(groups * GROUP // cols):
        lanes = slice(block * cols, min(width, (block + 1) * cols))
        group = block * cols // GROUP
        project_block(
            block, cols, x_ref[...], w_ref[:, lanes], valid_ref, z_ref, group * count, stat_ref, micro, width
        )


def project(inputs, weight, valid, micro, from_tiles):
    depth, width = weight.shape
    groups = groups_of(width)
    count = inputs.shape[0] // (groups * SUBS) if from_tiles else inputs.shape[0]
    cols = 512
    per_group = GROUP // cols
    stat_shape = (4 * micro * groups * SUBS, LANES)
    out_shape = [
        pltpu.VMEM((groups * count * SUBS, LANES), jnp.float32),
        pltpu.VMEM(stat_shape, jnp.float32),
    ]
    estimate = cost(2 * count * width * depth, weight.size * 2 + count * width * 6)
    if from_tiles:
        outs = pl.pallas_call(
            functools.partial(project_tiles_kernel, micro, cols),
            in_specs=[vmem()] * 3,
            out_specs=[vmem()] * 3,
            out_shape=out_shape + [pltpu.VMEM((count, depth), jnp.bfloat16)],
            compiler_params=limit(20),
            cost_estimate=estimate,
            name="project_tiles",
        )(valid, held(inputs), held(weight))
    else:
        outs = pl.pallas_call(
            functools.partial(project_rows_kernel, micro, cols),
            in_specs=[vmem(), anywhere(), anywhere()],
            out_specs=[vmem()] * 2,
            out_shape=out_shape,
            scratch_shapes=[
                pltpu.VMEM(inputs.shape, inputs.dtype),
                pltpu.VMEM(weight.shape, weight.dtype),
                pltpu.SemaphoreType.DMA((1 - (-width // cols),)),
            ],
            compiler_params=limit(53),
            cost_estimate=estimate,
            name="project_rows",
        )(valid, distant(inputs), distant(weight))
    stat = outs[1].reshape(4, micro, groups, SUBS, LANES)
    return (outs[0], stat) + tuple(outs[2:])


def combined_stats(parts):
    number = tree_sum([part[2] for part in parts])
    total = tree_sum([part[0] for part in parts])
    centre = total / jnp.maximum(number, 1.0)
    spread = tree_sum(
        [part[1] + part[2] * jnp.square(part[0] / jnp.maximum(part[2], 1.0) - centre) for part in parts]
    )
    return total, spread, number, tree_sum([part[3] for part in parts]), centre


def merge_kernel(*refs):
    merged = combined_stats([[ref[n] for n in range(4)] for ref in refs[:-1]])
    for n in range(4):
        refs[-1][n] = merged[n]


def merged_stats(parts):
    return pl.pallas_call(
        merge_kernel,
        in_specs=[vmem()] * len(parts),
        out_specs=vmem(),
        out_shape=jax.ShapeDtypeStruct(parts[0].shape, jnp.float32),
        compiler_params=limit(8),
        cost_estimate=cost(parts[0].size * 20, parts[0].size * 20),
        name="merge_stats",
    )(*parts)


def stat_parts(stat):
    rounds = [("rows", bit) for bit in bits_of("rows")] + [("tm", bit) for bit in bits_of("tm")]
    for axis, bit in rounds[:-1]:
        stat = merged_stats([stat, swapped(stat, axis, bit)])
    axis, bit = rounds[-1]
    return [stat, swapped(stat, axis, bit)]


def chain_kernel(
    sweep, send_end, layer, streams, micro, step, number_of_parts, total_frames, jobs, me_ref, reset_ref, z_ref, *refs
):
    parts, refs = refs[:number_of_parts], refs[number_of_parts:]
    vector_ref, entry_ref, last_ref, *refs = refs
    job_inputs, refs = [], list(refs)
    for job in jobs:
        job_inputs.append(refs[: job.inputs])
        refs = refs[job.inputs :]
    if sweep > 0:
        refs = refs[1 + len(jobs) :]
    s_ref, refs = refs[0], refs[1:]
    if send_end:
        end_ref, refs = refs[0], refs[1:]
    job_outputs, refs = refs[: len(jobs)], refs[len(jobs) :]
    if sweep == 0:
        norm_ref, refs = refs[0], refs[1:]
    lines, frames = z_ref.shape[0], z_ref.shape[1] // SUBS
    groups = lines // streams
    me = me_ref[0]

    def means_and_scales():
        centres, invs = {}, {}
        for m in range(micro):
            for g in range(groups):
                total, spread, number, inputs, centre = combined_stats(
                    [[part[n, m, g] for n in range(4)] for part in parts]
                )
                inv = lax.rsqrt(spread / number + EPSILON)
                centres[m, g], invs[m, g] = centre, inv
                if sweep == 0:
                    mean = inputs * (1.0 / total_frames)
                    for n, value in enumerate((centre, inv, number, mean)):
                        norm_ref[n, m, g] = value
        return centres, invs

    if sweep == 0:
        means_and_scales()

    @pl.when(me == sweep)
    def _():
        centres, invs = means_and_scales()
        per_micro = streams // micro
        keys = [(i % streams // per_micro, i // streams) for i in range(lines)]
        centre = [centres[key] for key in keys]
        scale = [invs[key] * (vector_ref[layer, key[1]] * LOG2E) for key in keys]
        shift = [vector_ref[layer + 2, g] * LOG2E for g in range(groups)]
        decay = [vector_ref[layer + 4, g] * LOG2E for g in range(groups)]

        def advance_piece(c, states):
            for k in range(step):
                t = c * step + k
                at = pl.ds(pl.multiple_of(t * SUBS, SUBS), SUBS)
                keep = [
                    jnp.where(reset_ref[r // per_micro, r % per_micro, t] == 0, 1.0, 0.0)
                    for r in range(streams)
                ]
                updated = []
                for i in range(lines):
                    g = i // streams
                    level = (z_ref[i, at, :] - centre[i]) * scale[i] + shift[g]
                    act = level + (decay[g] * keep[i % streams]) * states[i]
                    state = jnp.where(act > 64.0, act * LN2, jnp.log(1.0 + jnp.exp2(act)))
                    s_ref[i, at, :] = state
                    updated.append(state)
                states = tuple(updated)
            return states

        states = lax.fori_loop(
            0, frames // step, advance_piece, tuple(entry_ref[i] for i in range(lines))
        )
        if send_end:
            for i in range(lines):
                end_ref[i] = states[i]

    if send_end:

        @pl.when(me != sweep)
        def _():
            end_ref[...] = last_ref[...]

    turn = jnp.where(me < sweep, sweep - 1, sweep)
    for number, job in enumerate(jobs):
        if number > sweep:
            continue

        @pl.when((me != sweep) & (turn == number))
        def _(job=job, number=number):
            scratch, sems = [refs[at] for at in job.scratch], refs[-1]
            means = lambda m, g: tree_sum([part[3, m, g] for part in parts]) * (1.0 / total_frames)
            job.work(job_inputs[number], job_outputs[number], scratch, sems, means)


class TurnJob:
    inputs = 1
    specs = [anywhere()]

    def __init__(self, rows, micro):
        frames, width = rows.shape
        self.micro = micro
        count = lax.axis_size("tm")
        self.real, self.deep = group_rows(width, count, micro)
        self.operands = [rows]
        self.out = pltpu.HBM((count * self.deep, frames + ROWS16), jnp.bfloat16)
        self.buffers = [
            pltpu.VMEM(rows.shape, jnp.bfloat16),
            pltpu.VMEM((count * self.deep, frames + ROWS16), jnp.bfloat16),
            pltpu.VMEM((frames + ROWS16, self.deep // 2), jnp.float32),
            pltpu.VMEM((ROWS16, groups_of(width) * GROUP), jnp.float32),
        ]

    def work(self, inputs, out_hbm, scratch, sems, means):
        x_ref, turned_ref, buffer_ref, aug_ref = scratch
        load = pltpu.make_async_copy(inputs[0], x_ref, sems.at[0])
        load.start()
        aug_ref[...] = jnp.zeros_like(aug_ref)
        for g in range(aug_ref.shape[1] // GROUP):
            for m in range(self.micro):
                mean = means(m, g).astype(jnp.bfloat16).astype(jnp.float32)
                for sub in range(SUBS):
                    lanes = slice((g * SUBS + sub) * LANES, (g * SUBS + sub + 1) * LANES)
                    aug_ref[SPLIT * m : SPLIT * (m + 1), lanes] = jnp.broadcast_to(
                        mean[sub : sub + 1, :], (SPLIT, LANES)
                    )
        frames, width = x_ref.shape
        half = self.deep // 2
        groups = width // self.real
        pad = self.deep - self.real
        row = lax.broadcasted_iota(jnp.int32, (frames + ROWS16, pad), 0)
        col = lax.broadcasted_iota(jnp.int32, (frames + ROWS16, pad), 1)
        ones = jnp.zeros((frames + ROWS16, pad), jnp.float32)
        for m in range(self.micro):
            span = frames // self.micro
            rows_in = (row >= m * span) & (row < (m + 1) * span)
            ones = jnp.where(rows_in & (col >= SPLIT * m) & (col < SPLIT * (m + 1)), 1.0, ones)
        load.wait()
        for path in range(2):
            wide = half if path == 0 else half - pad
            if path == 1:
                buffer_ref[:, wide:] = ones
            for group in range(groups):
                first_lane = group * self.real + path * half
                lanes = slice(first_lane, first_lane + wide)
                buffer_ref[:frames, :wide] = x_ref[:, lanes].astype(jnp.float32)
                buffer_ref[frames:, :wide] = aug_ref[:, lanes]
                first = (path * groups + group) * half
                turned_ref[first : first + half, :] = buffer_ref[...].T.astype(jnp.bfloat16)
        store = pltpu.make_async_copy(turned_ref, out_hbm, sems.at[1])
        store.start()
        store.wait()


class TilesJob:
    inputs = 1
    specs = [anywhere()]

    def __init__(self, rows):
        count, width = rows.shape
        self.operands = [rows]
        self.out = pltpu.HBM((groups_of(width) * count * SUBS, LANES), jnp.float32)
        self.buffers = [
            pltpu.VMEM(rows.shape, jnp.bfloat16),
            pltpu.VMEM((groups_of(width) * count * SUBS, LANES), jnp.float32),
        ]

    def work(self, inputs, out_hbm, scratch, sems, means):
        x_ref, tiles_ref = scratch
        load = pltpu.make_async_copy(inputs[0], x_ref, sems.at[0])
        load.start()
        load.wait()
        count, width = x_ref.shape
        for tile in range(groups_of(width) * SUBS):
            group, sub = divmod(tile, SUBS)
            wide = max(0, min(LANES, width - tile * LANES))
            part = jnp.zeros((count, LANES), jnp.float32)
            if wide > 0:
                part = x_ref[:, tile * LANES : tile * LANES + wide].astype(jnp.float32)
            if 0 < wide < LANES:
                part = jnp.concatenate([part, jnp.zeros((count, LANES - wide), jnp.float32)], axis=1)
            tiles_ref[pl.ds(group * count * SUBS + sub, count, stride=SUBS), :] = part
        store = pltpu.make_async_copy(tiles_ref, out_hbm, sems.at[1])
        store.start()
        store.wait()


def chain(sweep, send_end, layer, resets, z, parts, vectors, entry, last, states, jobs, made, total_frames):
    lines, rows = z.shape[0], z.shape[1]
    streams = resets.shape[0] * resets.shape[1]
    micro = parts[0].shape[1]
    step = piece_size(rows // SUBS, 44)
    scratch, places = [], {}
    for job in jobs:
        job.scratch = []
        for buffer in job.buffers:
            form = (buffer.shape, buffer.dtype)
            if form not in places:
                places[form] = len(scratch)
                scratch.append(buffer)
            job.scratch.append(places[form])
    room = sum(math.prod(buffer.shape) * buffer.dtype.itemsize for buffer in scratch) >> 20
    out_shape = [pltpu.VMEM(z.shape, jnp.float32)]
    if send_end:
        out_shape.append(pltpu.VMEM((lines, SUBS, LANES), jnp.float32))
    first_job = len(out_shape)
    out_specs = [vmem()] * first_job + [anywhere()] * len(jobs)
    out_shape += [job.out for job in jobs]
    operands = [lax.axis_index("tm").reshape(1), resets, held(z)]
    operands += [*parts, vectors, entry, last]
    in_specs = [smem()] * 2 + [vmem()] * (len(operands) - 2)
    for job in jobs:
        operands += job.operands
        in_specs += job.specs
    aliases = {}
    if sweep == 0:
        out_shape.append(jax.ShapeDtypeStruct(parts[0].shape, jnp.float32))
        out_specs.append(vmem())
    else:
        aliases = {len(operands): 0}
        aliases |= {len(operands) + 1 + n: first_job + n for n in range(len(jobs))}
        operands += [held(states)] + [distant(array) for array in made]
        in_specs += [vmem()] + [anywhere()] * len(jobs)
    return pl.pallas_call(
        functools.partial(
            chain_kernel, sweep, send_end, layer, streams, micro, step, len(parts), total_frames, jobs
        ),
        in_specs=in_specs,
        out_specs=out_specs,
        out_shape=out_shape,
        scratch_shapes=scratch + [pltpu.SemaphoreType.DMA((2,))],
        input_output_aliases=aliases,
        compiler_params=limit(24),
        cost_estimate=cost(z.size * 200, z.size * 8, z.size * 2),
        name="chain",
    )(*operands)


def forward_layer(layer, z, parts, vectors, zeros, resets, total_frames, jobs):
    streams, frames = resets.shape[0] * resets.shape[1], resets.shape[2]
    z = z.reshape(-1, frames * SUBS, LANES)
    entry = last = zeros
    states, made = None, None
    for sweep in range(lax.axis_size("tm")):
        if sweep > 0:
            entry = shifted(last, "tm", 1)
        send_end = sweep < lax.axis_size("tm") - 1
        states, *made = chain(
            sweep, send_end, layer, resets, z, parts, vectors, entry, last, states, jobs, made, total_frames
        )
        if send_end:
            last, *made = made
        if sweep == 0:
            norm = made.pop()
    return dict(
        z=z,
        states=states,
        norm=norm,
        entry=entry,
        layer=layer,
        vectors=vectors,
    ), made


def retreat_kernel(
    layer, squares, streams, micro, flag_ref, z_ref, s_ref, d_ref, norm_ref, vector_ref, entry_ref,
    grad_ref, mult_ref, sums_ref, kept_ref, *square_refs,
):
    lines, frames = z_ref.shape[0], z_ref.shape[1] // SUBS
    groups = lines // streams
    per_micro = streams // micro
    zero = jnp.zeros((SUBS, LANES), jnp.float32)
    one = jnp.ones((SUBS, LANES), jnp.float32)
    for g in range(groups):
        centre = [norm_ref[0, r // per_micro, g] for r in range(streams)]
        inv = [norm_ref[1, r // per_micro, g] for r in range(streams)]
        decay = vector_ref[layer + 4, g]

        def at_frame(t, previous, carry):
            at = pl.ds(pl.multiple_of(t * SUBS, SUBS), SUBS)
            updated = []
            for r in range(streams):
                i = g * streams + r
                keep = flag_ref[0, r, t]
                lead, grow, *sums = carry[r]
                state = s_ref[i, at, :]
                slope = 1.0 - jnp.exp2(state * (-LOG2E))
                grad = slope * (d_ref[i, at, :] + lead)
                mult = slope * grow
                grad_ref[i, at, :] = grad
                mult_ref[i, at, :] = mult
                normed = (z_ref[i, at, :] - centre[r]) * inv[r]
                kept = previous(i) * keep
                terms = (grad, mult, grad * normed, mult * normed, grad * kept, mult * kept)
                if squares:
                    terms += (state * state * flag_ref[1, r, t],)
                rate = decay * keep
                updated.append(
                    (rate * grad, rate * mult)
                    + tuple(total + term for total, term in zip(sums, terms))
                )
            return tuple(updated)

        def body(k, carry):
            t = frames - 1 - k
            before = pl.ds(pl.multiple_of((t - 1) * SUBS, SUBS), SUBS)
            return at_frame(t, lambda i: s_ref[i, before, :], carry)

        carry = tuple((zero, one) + (zero,) * (7 if squares else 6) for _ in range(streams))
        carry = lax.fori_loop(0, frames - 1, body, carry, unroll=9 if frames % 9 == 1 else 5)
        carry = at_frame(0, lambda i: entry_ref[i], carry)
        for r in range(streams):
            for n in range(6):
                sums_ref[n, g * streams + r] = carry[r][n]
            for n in range(2):
                kept_ref[n, g * streams + r] = carry[r][6 + n]
        if squares:
            square_refs[0][g] = tree_sum([carry[r][8] for r in range(streams)])


def retreat(flags, fwd, grad_states, squares):
    z, states = fwd["z"], fwd["states"]
    lines = z.shape[0]
    streams = flags.shape[1]
    micro = fwd["norm"].shape[1]
    vector = lambda planes: jax.ShapeDtypeStruct((planes, lines, SUBS, LANES), jnp.float32)
    out_shape = [
        pltpu.VMEM(z.shape, jnp.float32),
        pltpu.VMEM(z.shape, jnp.float32),
        vector(6),
        pltpu.HBM((2, lines, SUBS, LANES), jnp.float32),
    ]
    if squares:
        out_shape.append(jax.ShapeDtypeStruct((lines // streams, SUBS, LANES), jnp.float32))
    return pl.pallas_call(
        functools.partial(retreat_kernel, fwd["layer"], squares, streams, micro),
        in_specs=[smem()] + [vmem()] * 6,
        out_specs=[vmem()] * len(out_shape),
        out_shape=out_shape,
        compiler_params=limit(6),
        cost_estimate=cost(z.size * 150, z.size * 20, z.size * 2),
        name="retreat",
    )(flags, held(z), held(states), held(grad_states), fwd["norm"], fwd["vectors"], fwd["entry"])


def compose_kernel(bit, me_ref, mine_ref, got_ref, lead_ref, map_ref, out_lead_ref):
    earlier_is_mine = (me_ref[0] // bit) % 2 == 0
    for i in range(mine_ref.shape[1]):
        mine = [mine_ref[n, i] for n in range(6)]
        got = [got_ref[n, i] for n in range(6)]
        early = [jnp.where(earlier_is_mine, a, b) for a, b in zip(mine, got)]
        late = [jnp.where(earlier_is_mine, b, a) for a, b in zip(mine, got)]
        map_ref[0, i] = early[0] + early[1] * late[0]
        map_ref[1, i] = early[1] * late[1]
        for n in (2, 4):
            map_ref[n, i] = early[n] + early[n + 1] * late[0] + late[n]
            map_ref[n + 1, i] = early[n + 1] * late[1] + late[n + 1]
        constant, factor = lead_ref[0, i], lead_ref[1, i]
        out_lead_ref[0, i] = jnp.where(earlier_is_mine, constant + factor * got[0], constant)
        out_lead_ref[1, i] = jnp.where(earlier_is_mine, factor * got[1], factor)


def composed(me, maps, lead, bit):
    shape = lambda array: jax.ShapeDtypeStruct(array.shape, jnp.float32)
    return pl.pallas_call(
        functools.partial(compose_kernel, bit),
        in_specs=[smem()] + [vmem()] * 3,
        out_specs=[vmem()] * 2,
        out_shape=[shape(maps), shape(lead)],
        compiler_params=limit(4),
        cost_estimate=cost(maps.size * 20, maps.size * 20),
        name="compose",
    )(me, maps, swapped(maps, "tm", bit), lead)


def totals_kernel(streams, micro, maps_ref, kept_ref, lead_ref, *refs):
    more_refs, out_ref = refs[:-1], refs[-1]
    groups = maps_ref.shape[1] // streams
    per_micro = streams // micro
    at = 0
    for n in range(2):
        for m in range(micro):
            for g in range(groups):
                first = g * streams + m * per_micro
                out_ref[at] = sum(maps_ref[2 + 2 * n, first + r] for r in range(per_micro))
                at += 1
    for g in range(groups):
        out_ref[at] = sum(
            kept_ref[0, i] + kept_ref[1, i] * lead_ref[0, i]
            for i in range(g * streams, (g + 1) * streams)
        )
        at += 1
    for ref in more_refs:
        for n in range(ref.shape[0]):
            out_ref[at] = ref[n]
            at += 1


def totals(maps, kept, lead, streams, micro, more):
    groups = maps.shape[1] // streams
    count = groups * (2 * micro + 1) + sum(tiles.shape[0] for tiles in more)
    return pl.pallas_call(
        functools.partial(totals_kernel, streams, micro),
        in_specs=[vmem()] * (3 + len(more)),
        out_specs=vmem(),
        out_shape=jax.ShapeDtypeStruct((count, SUBS, LANES), jnp.float32),
        compiler_params=limit(8),
        cost_estimate=cost(maps.size, maps.size * 4),
        name="totals",
    )(maps, kept, lead, *more)


def add_kernel(one_ref, two_ref, out_ref):
    out_ref[...] = one_ref[...] + two_ref[...]


def added(one, two):
    return pl.pallas_call(
        add_kernel,
        in_specs=[vmem()] * 2,
        out_specs=vmem(),
        out_shape=jax.ShapeDtypeStruct(one.shape, one.dtype),
        compiler_params=limit(6),
        cost_estimate=cost(one.size, one.size * 12),
        name="added",
    )(one, two)


def split_rows(value, first, micro):
    high = value.astype(jnp.bfloat16).astype(jnp.float32)
    rest = value - high
    middle = rest.astype(jnp.bfloat16).astype(jnp.float32)
    row = lax.broadcasted_iota(jnp.int32, value.shape, 0)
    part = lax.rem(row - first + 3 * ROWS16, SPLIT)
    inside = (row >= first) & (row < first + SPLIT * micro)
    value = jnp.where(inside & (part == 1), middle, high)
    return jnp.where(inside & (part == 2), rest - middle, value)


def grad_kernel(
    layer, streams, micro, with_whole, group_ref, valid_ref, z_ref, grad_ref, mult_ref,
    norm_ref, vector_ref, lead_ref, total_ref, *refs,
):
    groups = z_ref.shape[0] // streams
    if with_whole:
        other_ref, out_ref, whole_ref, tile_ref = refs
    else:
        out_ref, tile_ref = refs
    frames = z_ref.shape[1] // SUBS
    per_micro = streams // micro
    g = group_ref[0]
    sums = [
        [total_ref[(n * micro + m) * groups + g] / norm_ref[2, m, g] for n in range(2)]
        for m in range(micro)
    ]
    centre = [norm_ref[0, m, g] for m in range(micro)]
    inv = [norm_ref[1, m, g] for m in range(micro)]
    scale = [inv[m] * vector_ref[layer, g] for m in range(micro)]
    lead = [lead_ref[0, g * streams + r] for r in range(streams)]

    def body(t, carried):
        at = pl.ds(pl.multiple_of(t * SUBS, SUBS), SUBS)
        for r in range(streams):
            m = r // per_micro
            i = g * streams + r
            normed = (z_ref[i, at, :] - centre[m]) * inv[m]
            act_grad = grad_ref[i, at, :] + mult_ref[i, at, :] * lead[r]
            common = sums[m][0] + normed * sums[m][1]
            tile_ref[pl.ds(pl.multiple_of((r * frames + t) * SUBS, SUBS), SUBS), :] = scale[m] * (
                act_grad - jnp.where(valid_ref[m, r % per_micro, t] == 0, 0.0, 1.0) * common
            )
        return carried

    lax.fori_loop(0, frames, body, 0, unroll=16)
    count = streams * frames
    span = count // micro
    for sub in range(SUBS):
        lanes = slice(sub * LANES, (sub + 1) * LANES)
        rows = [jnp.zeros((1, LANES), jnp.float32)] * ROWS16
        for m in range(micro):
            part = tile_ref[pl.ds(m * span * SUBS + sub, span, stride=SUBS), :].astype(jnp.bfloat16)
            out_ref[m * span : (m + 1) * span, lanes] = part
            total = -jnp.sum(part.astype(jnp.float32), axis=0, keepdims=True)
            rows[SPLIT * m : SPLIT * (m + 1)] = [total] * SPLIT
        out_ref[count : count + ROWS16, lanes] = split_rows(
            jnp.concatenate(rows, axis=0), 0, micro
        ).astype(jnp.bfloat16)
    if with_whole:
        whole_ref[:, pl.ds(pl.multiple_of(g * GROUP, GROUP), GROUP)] = out_ref[:count, :]
        whole_ref[:, pl.ds(pl.multiple_of((1 - g) * GROUP, GROUP), GROUP)] = other_ref[:count, :]


def projection_grad(group, valid, fwd, grad, mult, lead, total, other, whole_space):
    z = fwd["z"]
    streams, frames = valid.shape[0] * valid.shape[1], z.shape[1] // SUBS
    micro = fwd["norm"].shape[1]
    count = streams * frames
    out_shape = [pltpu.VMEM((count + ROWS16, GROUP), jnp.bfloat16)]
    others = []
    if other is not None:
        others = [held(other)]
        out_shape.append(whole_space((count, 2 * GROUP), jnp.bfloat16))
    return pl.pallas_call(
        functools.partial(grad_kernel, fwd["layer"], streams, micro, other is not None),
        in_specs=[smem()] * 2 + [vmem()] * (7 + len(others)),
        out_specs=[vmem()] * len(out_shape),
        out_shape=out_shape,
        scratch_shapes=[pltpu.VMEM((count * SUBS, LANES), jnp.float32)],
        compiler_params=limit(10),
        cost_estimate=cost(z.size * 25, z.size * 8),
        name="projection_grad",
    )(group, valid, held(z), held(grad), held(mult), fwd["norm"], fwd["vectors"], lead, total, *others)


def input_grad_block(width, d_ref, w_ref):
    return lax.dot_general(
        d_ref[:, :width], w_ref[...], (((1,), (1,)), ((), ())), preferred_element_type=jnp.float32
    )


def input_grad_tiles_kernel(rows, d_ref, w_hbm, out_ref, w_ref, sems):
    width = w_ref.shape[0]
    count = d_ref.shape[0]
    blocks = [slice(at, min(width, at + rows)) for at in range(0, width, rows)]
    loads = [
        pltpu.make_async_copy(w_hbm.at[at, :], w_ref.at[at, :], sems.at[n])
        for n, at in enumerate(blocks)
    ]
    for load in loads[:2]:
        load.start()
    for block, at in enumerate(blocks):
        loads[block].wait()
        if block + 2 < len(blocks):
            loads[block + 2].start()
        grad = lax.dot_general(
            d_ref[:, :width], w_ref[at, :], (((1,), (1,)), ((), ())), preferred_element_type=jnp.float32
        )
        for q in range(rows // LANES):
            group, sub = divmod(block * rows // LANES + q, SUBS)
            wide = max(0, min(LANES, grad.shape[1] - q * LANES))
            part = grad[:, q * LANES : q * LANES + wide]
            if wide < LANES:
                part = jnp.concatenate([part, jnp.zeros((count, LANES - wide), jnp.float32)], axis=1)
            out_ref[pl.ds(group * count * SUBS + sub, count, stride=SUBS), :] = part


def input_grad_rows_kernel(width, d_ref, w_ref, add_ref, out_ref):
    out_ref[...] = input_grad_block(width, d_ref, w_ref) + add_ref[...].astype(jnp.float32)


def input_grad(grad, weight, added):
    width = weight.shape[0]
    count = grad.shape[0]
    groups = groups_of(width)
    rows = 512
    in_specs = [
        pl.BlockSpec(grad.shape, lambda j: (0, 0)),
        pl.BlockSpec((rows, width), lambda j: (j, 0)),
    ]
    estimate = cost(2 * count * width * width, weight.size * 2 + count * width * 8)
    if added is None:
        return pl.pallas_call(
            functools.partial(input_grad_tiles_kernel, rows),
            in_specs=[vmem(), anywhere()],
            out_specs=vmem(),
            out_shape=pltpu.VMEM((groups * count * SUBS, LANES), jnp.float32),
            scratch_shapes=[
                pltpu.VMEM(weight.shape, weight.dtype),
                pltpu.SemaphoreType.DMA((-(-width // rows),)),
            ],
            compiler_params=limit(20),
            cost_estimate=estimate,
            name="input_grad_tiles",
        )(held(grad), distant(weight))
    return pl.pallas_call(
        functools.partial(input_grad_rows_kernel, width),
        grid=(groups * GROUP // rows,),
        in_specs=in_specs + [pl.BlockSpec((count, rows), lambda j: (0, j))],
        out_specs=pl.BlockSpec((count, rows), lambda j: (0, j)),
        out_shape=jax.ShapeDtypeStruct((count, width), jnp.float32),
        compiler_params=limit(54),
        cost_estimate=estimate,
        name="input_grad_rows",
    )(grad, weight, added)


def output_kernel(s_ref, x_ref, out_ref):
    step, width = x_ref.shape
    for tile in range(-(-width // LANES)):
        group, sub = divmod(tile, SUBS)
        wide = min(LANES, width - tile * LANES)
        lanes = slice(tile * LANES, tile * LANES + wide)
        state = s_ref[group, 0, pl.ds(sub, step, stride=SUBS), :]
        out_ref[:, lanes] = x_ref[:, lanes].astype(jnp.float32) + state[:, :wide]


def block_output(states, inputs, streams):
    count, width = inputs.shape
    frames = count // streams
    groups = states.shape[0] // streams
    step = frames // 2 if frames % (2 * ROWS16) == 0 else frames
    pieces = frames // step
    tiles = states.reshape(groups, streams, frames * SUBS, LANES)
    rows = pl.BlockSpec((step, width), lambda r, c: (r * pieces + c, 0))
    return pl.pallas_call(
        output_kernel,
        grid=(streams, pieces),
        in_specs=[pl.BlockSpec((groups, 1, step * SUBS, LANES), lambda r, c: (0, r, c, 0)), rows],
        out_specs=rows,
        out_shape=jax.ShapeDtypeStruct((count, width), jnp.float32),
        compiler_params=limit(10),
        cost_estimate=cost(states.size * 6, states.size * 10),
        name="block_output",
    )(distant(tiles), distant(inputs))


def group_rows(width, count, micro):
    rows = width // count
    deep = -(-(rows + SPLIT * micro) // (2 * ROWS16)) * 2 * ROWS16
    return rows, deep


def share_kernel(micro, first, groups, bits_ref, own_x, got_x, own_d, got_d, *out_refs):
    total = jnp.dot(own_x[...], own_d[...], preferred_element_type=jnp.float32) + jnp.dot(
        got_x[...], got_d[...], preferred_element_type=jnp.float32
    )
    if len(out_refs) == 1:
        out_refs[0][...] = total
        return
    half = total.shape[0] // groups
    sides = len(out_refs) // 2
    for n, out_ref in enumerate(out_refs):
        path, side = divmod(n, sides)
        turn = pl.program_id(0) == path
        if sides > 1:
            turn = turn & (pl.program_id(1) == side)

        @pl.when(turn)
        def _(out_ref=out_ref, path=path):
            out_ref[...] = total.astype(jnp.bfloat16)
            if path == 1:
                for group in range(groups):
                    at = slice((group + 1) * half - ROWS16, (group + 1) * half)
                    out_ref[at, :] = split_rows(total[at, :], first, micro).astype(jnp.bfloat16)


def weight_share(bits, own_x, got_x, own_d, got_d, micro, groups, first, sent, split=False):
    rows = own_x.shape[0] // 2
    depth = own_x.shape[1]
    cut = own_d.shape[1] // 4

    def columns(path, side, bits):
        return (0, jnp.where(path == 0, 2 * bits[0] + side, 2 * side + bits[1]))

    x_spec = pl.BlockSpec((rows, depth), lambda path, side, bits: (path, 0))
    d_spec = pl.BlockSpec((depth, cut), columns)
    if split:
        out_specs = [pl.BlockSpec((rows, cut), lambda path, side, bits: (0, 0))] * 4
        out_shape = [jax.ShapeDtypeStruct((rows, cut), jnp.bfloat16)] * 4
    elif sent:
        out_specs = [
            pl.BlockSpec((None, rows, cut), lambda path, side, bits: (jnp.where(path == 0, side, 1), 0, 0)),
            pl.BlockSpec((None, rows, cut), lambda path, side, bits: (jnp.where(path == 0, 0, side), 0, 0)),
        ]
        out_shape = [jax.ShapeDtypeStruct((2, rows, cut), jnp.bfloat16)] * 2
    else:
        out_specs = pl.BlockSpec(
            (None, None, rows, cut), lambda path, side, bits: (path, side, 0, 0)
        )
        out_shape = jax.ShapeDtypeStruct((2, 2, rows, cut), jnp.float32)
    return pl.pallas_call(
        functools.partial(share_kernel, micro, first, groups),
        grid_spec=pltpu.PrefetchScalarGridSpec(
            num_scalar_prefetch=1,
            grid=(2, 2),
            in_specs=[x_spec, x_spec, d_spec, d_spec],
            out_specs=out_specs,
        ),
        out_shape=out_shape,
        compiler_params=limit(20),
        cost_estimate=cost(4 * rows * 2 * depth * cut * 4, own_x.size * 8),
        name="share_sent" if sent else "share_kept",
    )(bits, distant(own_x), distant(got_x), own_d, got_d)


def added_tail(own, gots, first, micro):
    rows = [own[n : n + 1, :] for n in range(ROWS16)]
    news = [[got[n : n + 1, :] for n in range(ROWS16)] for got in gots]
    result = [tree_sum([rows[n]] + [new[n] for new in news]) for n in range(ROWS16)]
    for m in range(micro):
        at = first + SPLIT * m
        total = tree_sum([rows[at]] + [new[at] + new[at + 1] + new[at + 2] for new in news])
        result[at : at + SPLIT] = [total] * SPLIT
    return jnp.concatenate(result, axis=0)


def halve_kernel(micro, first, groups, bits_ref, kept_ref, *refs):
    got_refs, (send0_ref, send1_ref, keep_ref) = refs[:-3], refs[-3:]
    half = kept_ref.shape[2] // groups
    body = half - ROWS16
    for path, send_ref in enumerate((send0_ref, send1_ref)):
        mine = bits_ref[1 - path]
        for side in range(2):
            if len(got_refs) == 2:
                got_ref, lead = got_refs[path], (side,)
            else:
                got_ref, lead = got_refs[2 * path + side], ()

            def values(path=path, side=side, got_ref=got_ref, lead=lead):
                for group in range(groups):
                    start = group * half
                    if path == 0:
                        at = pl.ds(start, half)
                        yield at, None, kept_ref[path, side, at, :] + got_ref[lead + (at, slice(None))].astype(
                            jnp.float32
                        )
                        continue
                    at = pl.ds(start, body)
                    tail = pl.ds(start + body, ROWS16)
                    value = kept_ref[path, side, at, :] + got_ref[lead + (at, slice(None))].astype(jnp.float32)
                    last = added_tail(
                        kept_ref[path, side, tail, :],
                        [got_ref[lead + (tail, slice(None))].astype(jnp.float32)],
                        first,
                        micro,
                    )
                    yield at, None, value
                    yield tail, True, last

            @pl.when(mine == side)
            def _(path=path, values=values):
                for at, _, value in values():
                    keep_ref[path, at, :] = value

            @pl.when(mine != side)
            def _(send_ref=send_ref, values=values):
                for at, is_tail, value in values():
                    if is_tail:
                        value = split_rows(value, first, micro)
                    send_ref[at, :] = value.astype(jnp.bfloat16)


def halve(bits, kept, gots, micro, groups, first):
    _, _, rows, cut = kept.shape
    low = jax.ShapeDtypeStruct((rows, cut), jnp.bfloat16)
    return pl.pallas_call(
        functools.partial(halve_kernel, micro, first, groups),
        in_specs=[smem()] + [vmem()] * (1 + len(gots)),
        out_specs=[vmem()] * 3,
        out_shape=[low, low, jax.ShapeDtypeStruct((2, rows, cut), jnp.float32)],
        compiler_params=limit(20),
        cost_estimate=cost(kept.size * 2, kept.size * 6),
        name="halve",
    )(bits, kept, *gots)


def spread_kernel(micro, first, groups, lanes, me_ref, kept_ref, got0_ref, got1_ref, keep_ref, send_ref):
    half = kept_ref.shape[1] // groups
    body = half - ROWS16
    mine = me_ref[0] % 2
    for pair in range(groups // 2):
        for is_kept, bit in ((False, 1 - mine), (True, mine)):
            start = (2 * pair + bit) * half
            at0 = pl.ds(pl.multiple_of(start, half), half)
            at1 = pl.ds(pl.multiple_of(start, half), body)
            tail = pl.ds(pl.multiple_of(start + body, ROWS16), ROWS16)
            low = kept_ref[0, at0, lanes] + got0_ref[at0, lanes].astype(jnp.float32)
            high = kept_ref[1, at1, lanes] + got1_ref[at1, lanes].astype(jnp.float32)
            last = added_tail(
                kept_ref[1, tail, lanes], [got1_ref[tail, lanes].astype(jnp.float32)], first, micro
            )
            out_ref = keep_ref if is_kept else send_ref
            if not is_kept:
                last = split_rows(last, first, micro)
            out_ref[pair, :half, :] = low.astype(out_ref.dtype)
            out_ref[pair, half : half + body, :] = high.astype(out_ref.dtype)
            out_ref[pair, half + body :, :] = last.astype(out_ref.dtype)


def halved(groups, deep, cut):
    shape = (groups // 2, deep, cut)
    return [jax.ShapeDtypeStruct(shape, jnp.float32), jax.ShapeDtypeStruct(shape, jnp.bfloat16)]


def spread(me, kept, got0, got1, micro, groups, first, chunk, chunks):
    _, rows, cut = kept.shape
    wide = cut // chunks
    lanes = slice(chunk * wide, (chunk + 1) * wide)
    return pl.pallas_call(
        functools.partial(spread_kernel, micro, first, groups, lanes),
        in_specs=[smem()] + [vmem()] * 3,
        out_specs=[vmem()] * 2,
        out_shape=halved(groups, 2 * rows // groups, wide),
        compiler_params=limit(16),
        cost_estimate=cost(kept.size * 2, kept.size * 8),
        name="spread",
    )(me, kept, got0, got1)


def narrow_kernel(micro, first, bit, me_ref, kept_ref, got_ref, keep_ref, send_ref):
    groups, deep, _ = kept_ref.shape
    body = deep - ROWS16
    mine = me_ref[0] // bit % 2
    for pair in range(groups // 2):
        for is_kept, at in ((False, 2 * pair + 1 - mine), (True, 2 * pair + mine)):
            value = kept_ref[at, :body, :] + got_ref[at, :body, :].astype(jnp.float32)
            last = added_tail(
                kept_ref[at, body:, :], [got_ref[at, body:, :].astype(jnp.float32)], first, micro
            )
            out_ref = keep_ref if is_kept else send_ref
            if not is_kept:
                last = split_rows(last, first, micro)
            out_ref[pair, :body, :] = value.astype(out_ref.dtype)
            out_ref[pair, body:, :] = last.astype(out_ref.dtype)


def narrow(me, kept, got, micro, first, bit):
    groups, deep, cut = kept.shape
    return pl.pallas_call(
        functools.partial(narrow_kernel, micro, first, bit),
        in_specs=[smem()] + [vmem()] * 2,
        out_specs=[vmem()] * 2,
        out_shape=halved(groups, deep, cut),
        compiler_params=limit(16),
        cost_estimate=cost(kept.size * 2, kept.size * 8),
        name="narrow",
    )(me, kept, got)


def gather_kernel(micro, first, real, final, with_before, me_ref, norm_ref, own_ref, got_ref, *refs):
    owns, gots = [own_ref], [got_ref]
    if with_before:
        before_ref, refs = refs[0], refs[1:]
    deep = owns[0].shape[0]
    body = deep - ROWS16
    sums = []
    for own_ref, got_ref in zip(owns, gots):
        value = own_ref[:body, :] + got_ref[:body, :].astype(jnp.float32)
        last = added_tail(own_ref[body:, :], [got_ref[body:, :].astype(jnp.float32)], first, micro)
        sums.append((value, last))
    if not final:
        out_ref, low_ref = refs
        value, last = sums[0]
        out_ref[:body, :] = value
        out_ref[body:, :] = last
        low_ref[:body, :] = value.astype(jnp.bfloat16)
        low_ref[body:, :] = split_rows(last, first, micro).astype(jnp.bfloat16)
        return
    out_refs, (lanes_ref, mean_ref) = refs[:-2], refs[-2:]
    groups = norm_ref.shape[2]
    mean_ref[...] = jnp.zeros_like(mean_ref)
    for m in range(micro):
        for g in range(groups):
            mean = norm_ref[3, m, g].astype(jnp.bfloat16).astype(jnp.float32)
            for sub in range(SUBS):
                lanes = slice((g * SUBS + sub) * LANES, (g * SUBS + sub + 1) * LANES)
                lanes_ref[m : m + 1, lanes] = mean[sub : sub + 1, :]
    for block in range(groups * GROUP // real):

        @pl.when(me_ref[0] == block)
        def _(block=block):
            mean_ref[:, :real] = lanes_ref[:, block * real : (block + 1) * real]

    wide = out_refs[0].shape[0]
    at_row = 0
    if with_before:
        at_row = before_ref.shape[0]
        out_refs[0][:at_row, :] = before_ref[...]
    for value, last in sums:
        turned = jnp.concatenate([value, last], axis=0).T
        for m in range(micro):
            at = body + first + SPLIT * m
            turned = turned + turned[:, at : at + 1] * mean_ref[m : m + 1, :]
        turned = turned.astype(jnp.bfloat16)
        for start in range(0, turned.shape[0], LANES):
            rows = turned[start : start + LANES, :]
            part, to = divmod(at_row, wide)
            out_refs[part][to : to + rows.shape[0], :] = rows
            at_row += rows.shape[0]


def gather_sum(me, norm, own, got, before, micro, first, real, final, parts=1):
    deep, cut = own.shape
    if before is not None:
        cut += before.shape[0]
    more = [] if before is None else [before]
    scratch = []
    if final:
        out_shape = [jax.ShapeDtypeStruct((cut // parts, deep), jnp.bfloat16)] * parts
        scratch = [
            pltpu.VMEM((SUBS, norm.shape[2] * GROUP), jnp.float32),
            pltpu.VMEM((SUBS, deep), jnp.float32),
        ]
    else:
        out_shape = [jax.ShapeDtypeStruct(own.shape, dtype) for dtype in (jnp.float32, jnp.bfloat16)]
    return pl.pallas_call(
        functools.partial(gather_kernel, micro, first, real, final, before is not None),
        in_specs=[smem()] + [vmem()] * (3 + len(more)),
        out_specs=[vmem()] * len(out_shape),
        out_shape=out_shape,
        scratch_shapes=scratch,
        compiler_params=limit(8),
        cost_estimate=cost(deep * cut * 10, deep * cut * 12),
        name="gather_sum",
    )(me, norm, own, got, *more)


def stack_kernel(cut, slots_ref, *refs):
    pieces, out_ref = refs[:-1], refs[-1]
    at = 0
    for piece in pieces:
        for block in range(piece.shape[0] // cut):
            to = pl.ds(pl.multiple_of(slots_ref[at] * cut, cut), cut)
            out_ref[to, :] = piece[block * cut : (block + 1) * cut, :]
            at += 1


def stacked(slots, pieces, cut):
    rows, deep = sum(piece.shape[0] for piece in pieces), pieces[0].shape[1]
    return pl.pallas_call(
        functools.partial(stack_kernel, cut),
        in_specs=[smem()] + [vmem()] * len(pieces),
        out_specs=vmem(),
        out_shape=jax.ShapeDtypeStruct((rows, deep), pieces[0].dtype),
        compiler_params=limit(8),
        cost_estimate=cost(rows * deep, rows * deep * 4),
        name="stacked",
    )(slots, *pieces)


def halves_kernel(per_half, core_ref, own_ref, got_ref, out_ref):
    mine = core_ref[0] == pl.program_id(0) // per_half
    rows = out_ref.shape[1]
    out_ref[...] = jnp.where(mine, own_ref[:, :rows], got_ref[:, :rows]).astype(jnp.float32)


def both_halves(core, own, got, rows, width):
    per_half = 2
    block = own.shape[0] // per_half
    half = pl.BlockSpec((block, own.shape[1]), lambda n: (n % per_half, 0))
    return pl.pallas_call(
        functools.partial(halves_kernel, per_half),
        grid=(2 * per_half,),
        in_specs=[smem(), half, half],
        out_specs=pl.BlockSpec((block, rows), lambda n: (n, 0)),
        out_shape=jax.ShapeDtypeStruct((width, rows), jnp.float32),
        compiler_params=limit(16),
        cost_estimate=cost(rows * width, rows * width * 6),
        name="both_halves",
    )(core, own, got)


class WeightGradSum:
    def __init__(self, places, turned, own_d, got_d, norm, width, chunks):
        self.places, self.x, self.d, self.norm, self.width = places, turned, (own_d, got_d), norm, width
        self.micro, self.count, self.chunks = norm.shape[1], lax.axis_size("tm"), chunks
        self.rows, self.deep = group_rows(width, self.count, self.micro)
        self.first = self.rows - (self.deep - ROWS16)

    def share(self, bits, sent, behind, split=False):
        own_d = after(self.d[0], behind)
        return weight_share(
            bits, *self.x, own_d, self.d[1], self.micro, self.count, self.first, sent, split
        )

    def make_sent(self, behind, split=False):
        self.sent = self.share(self.places["other_bits"], True, behind, split)
        self.got = [None] * len(self.sent)
        return self.sent[-1]

    def launch(self, behind, side=0):
        sides = len(self.sent) // 2
        for path, bit in enumerate((2, 4)):
            at = path * sides + side
            self.got[at] = swapped(after(self.sent[at], behind), "rows", bit)

    def make_kept(self, behind):
        self.kept = self.share(self.places["bits"], False, behind)
        return self.kept

    def make_halves(self, behind):
        send0, send1, self.kept = halve(
            self.places["bits"], after(self.kept, behind), self.got, self.micro, self.count, self.first
        )
        self.got = swapped(send0, "rows", 4), swapped(send1, "rows", 2)
        self.cut = self.kept.shape[2]
        return self.kept

    def make_spread(self, behind):
        kept, got, self.kept, self.got = after(self.kept, behind), self.got, [], []
        for chunk in range(self.chunks):
            keep, send = spread(
                self.places["me"], kept, *got, self.micro, self.count, self.first, chunk, self.chunks
            )
            kept = after(kept, keep)
            self.kept.append(keep)
            self.got.append(swapped(send, "tm", 1))
        return self.kept[-1]

    def make_narrow(self, behind, chunk=0):
        for bit in bits_of("tm")[1:]:
            keep, send = narrow(
                self.places["me"], after(self.kept[chunk], behind), self.got[chunk], self.micro, self.first, bit
            )
            self.kept[chunk], self.got[chunk] = keep, swapped(send, "tm", bit)
        return self.kept[chunk]

    def summed_piece(self, behind, chunk, before, parts):
        own, got = after(self.kept[chunk][0], behind), self.got[chunk][0]
        gather = functools.partial(
            gather_sum, self.places["me"], self.norm, micro=self.micro, first=self.first, real=self.rows
        )
        for bit in bits_of("rows")[3:]:
            own, send = gather(own, got, None, final=False)
            got = swapped(send, "rows", bit)
        return gather(own, got, before, final=True, parts=parts)

    def make_piece(self, behind, chunk):
        before = self.piece if chunk else None
        (self.piece,) = self.summed_piece(behind, chunk, before, 1)
        return self.piece

    def launch_piece(self, behind):
        piece = after(self.piece, behind)
        self.piece = [piece] + [swapped(piece, "rows", away) for away in (2, 4, 6)]

    def make_half(self, behind):
        piece = self.piece
        self.half = stacked(self.places["slots"], [after(piece[0], behind)] + piece[1:], piece[0].shape[0])
        self.other = swapped(self.half, "rows", 1)
        return self.half

    def make_two_pieces(self, behind):
        self.piece = self.summed_piece(behind, 0, None, 2)
        self.got = [swapped(piece, "rows", bit) for piece, bit in zip(self.piece, (4, 2))]
        return self.piece[1]

    def make_two_pairs(self, behind):
        piece = [after(value, behind) for value in self.piece]
        cut = piece[0].shape[0]
        slots = self.places["pair_slots"]
        self.piece = [stacked(slots[n], [piece[n], self.got[n]], cut) for n in range(2)]
        self.got = [swapped(pair, "rows", bit) for pair, bit in zip(self.piece, (2, 4))]
        return self.piece[1]

    def make_two_halves(self, behind):
        piece = [after(self.piece[0], behind), self.piece[1]]
        cut = piece[0].shape[0] // 2
        half = stacked(
            self.places["half_slots"], [piece[0], self.got[0], piece[1], self.got[1]], cut
        )
        self.half = half
        return half

    def launch_half(self, behind):
        self.half = after(self.half, behind)
        self.other = swapped(self.half, "rows", 1)

    def make_whole(self, behind):
        half = after(self.half, behind)
        return both_halves(self.places["core"], half, self.other, self.rows, self.width)


def backward_layer(grad_states, fwd, flags, squares, valid, places, during, more, whole_space):
    streams = flags.shape[1]
    micro = fwd["norm"].shape[1]
    grad, mult, maps, kept, *others = retreat(flags, fwd, grad_states, squares)
    during = list(during)
    lead = places["lead"]
    for bit in bits_of("tm"):
        if during:
            lead = after(lead, during.pop(0)(maps))
        maps, lead = composed(places["me"], maps, lead, bit)
    total = totals(maps, kept, lead, streams, micro, more)
    local = total
    for bit in bits_of("rows"):
        got = swapped(total, "rows", bit)
        if during:
            total = after(total, during.pop(0)(total))
        total = added(total, got)
    if during:
        total = after(total, during.pop(0)(total))
    make = functools.partial(
        projection_grad,
        valid=valid,
        fwd=fwd,
        grad=grad,
        mult=mult,
        lead=lead,
        total=total,
        whole_space=whole_space,
    )
    (theirs,) = make(places["other_core"], other=None)
    got = swapped(theirs, "rows", 1)
    own, whole = make(places["core"], other=theirs)
    return whole, own, got, local, total, others


def on_device(
    frames,
    resets,
    valid_frames,
    weight_one,
    gain_one,
    bias_one,
    decay_one,
    weight_two,
    gain_two,
    bias_two,
    decay_two,
    out_grad,
):
    micro, rows, span, width = frames.shape
    streams = micro * rows
    groups = groups_of(width)
    total_frames = rows * span * lax.axis_size("tm") * lax.axis_size("rows")
    row = lax.axis_index("rows")
    bits = jnp.stack([row // 2 % 2, row // 4 % 2])
    line = jnp.zeros((groups * streams, SUBS, LANES), jnp.float32)
    places = dict(
        me=lax.axis_index("tm").reshape(1),
        core=(row % 2).reshape(1),
        other_core=(1 - row % 2).reshape(1),
        bits=bits,
        other_bits=1 - bits,
        slots=jnp.stack([(row ^ away) // 2 % 2 * 2 + (row ^ away) // 4 % 2 for away in (0, 2, 4, 6)]),
        pair_slots=[jnp.stack([bits[1], 1 - bits[1]]), jnp.stack([bits[0], 1 - bits[0]])],
        half_slots=2 * jnp.stack(
            [2 * bits[0], 2 * bits[0] + 1, 2 - 2 * bits[0], 3 - 2 * bits[0]]
            + [bits[1], 2 + bits[1], 1 - bits[1], 3 - bits[1]]
        )
        + jnp.array([0] * 4 + [1] * 4),
        lead=jnp.stack([line, jnp.ones_like(line)]),
    )
    valid = valid_frames.reshape(streams, span)
    vectors = as_tiles(jnp.stack([gain_one, gain_two, bias_one, bias_two, decay_one, decay_two]))
    inputs, out_low = frames.reshape(-1, width), out_grad.reshape(-1, width)
    inputs, places, vectors, line = lax.optimization_barrier((inputs, places, vectors, line))

    z_one, stat_one = project(inputs, weight_one, valid, micro, False)
    inputs_got = swapped(inputs, "rows", 1)
    jobs = [TurnJob(distant(inputs), micro), TurnJob(inputs_got, micro), TilesJob(distant(out_low))]
    parts = stat_parts(stat_one)
    flags = jnp.stack([1 - after(resets, stat_one).reshape(streams, span), valid]).astype(jnp.float32)
    parts[0] = after(parts[0], flags)
    one, (*x_one, grad_tiles) = forward_layer(
        0, z_one, parts, vectors, line, resets, total_frames, jobs
    )
    z_two, stat_two, hidden = project(
        one["states"].reshape(-1, LANES), weight_two, valid, micro, True
    )
    parts = stat_parts(stat_two)
    hidden_got = swapped(after(hidden, parts[0]), "rows", 1)
    jobs = [TurnJob(hidden, micro), TurnJob(hidden_got, micro)]
    two, x_two = forward_layer(1, z_two, parts, vectors, line, resets, total_frames, jobs)

    whole, own_d, got_d, local_two, total_two, (square,) = backward_layer(
        grad_tiles.reshape(one["z"].shape), two, flags, True, valid_frames, places, [], [], pltpu.VMEM
    )
    sum_two = WeightGradSum(places, x_two, own_d, got_d, two["norm"], width, 1)
    done = sum_two.make_sent(whole)
    sum_two.launch(done)
    grad_hidden = input_grad(after(whole, done), weight_two, None).reshape(one["z"].shape)
    during = [sum_two.make_kept]
    during += [lambda behind: behind] * (len(bits_of("tm") + bits_of("rows")) - 1)
    during += [sum_two.make_halves]
    whole, own_d, got_d, _, total_one, _ = backward_layer(
        grad_hidden,
        one,
        flags,
        False,
        valid_frames,
        places,
        during,
        [local_two[groups * 2 * micro :], square],
        pltpu.HBM,
    )
    sum_one = WeightGradSum(places, x_one, own_d, got_d, one["norm"], width, 2)
    done = sum_one.make_sent(own_d)
    sum_one.launch(done)
    small = total_one[groups * 2 * micro :]
    rounds = bits_of("tm")
    small = added(after(small, done), swapped(small, "tm", rounds[0]))
    done = sum_two.make_spread(small)
    done = sum_one.make_kept(done)
    output = block_output(two["states"], after(inputs, done), streams)
    done = output
    for bit in rounds[1:]:
        small = added(after(small, done), swapped(small, "tm", bit))
    done = small

    small, total_one, total_two = after((small, total_one, total_two), done)
    number = jnp.sum(one["norm"][2, :, 0, 0, 0])
    vector = lambda tiles: tiles.reshape(-1)[:width]
    rms_value = jnp.sqrt(jnp.sum(vector(small[2 * groups :])) / (number * width))
    layer_sums = lambda total: total[: groups * 2 * micro].reshape(2, micro, -1).sum(axis=1)[:, :width]
    bias_grad_one, gain_grad_one = layer_sums(total_one)
    bias_grad_two, gain_grad_two = layer_sums(total_two)
    decay_grad_one, decay_grad_two = vector(small[:groups]), vector(small[groups : 2 * groups])
    vectors_made = (rms_value, bias_grad_one, gain_grad_one, bias_grad_two, gain_grad_two)
    done = after(done, *vectors_made, decay_grad_one, decay_grad_two)

    done = sum_two.make_narrow(done)
    done = sum_one.make_halves(done)
    input_gradient = input_grad(after(whole, done), weight_one, out_low)
    done = sum_one.make_spread(input_gradient)
    done = sum_two.make_two_pieces(done)
    done = sum_one.make_narrow(done, 0)
    done = sum_two.make_two_pairs(done)
    done = sum_one.make_narrow(done, 1)
    done = sum_one.make_piece(done, 0)
    done = sum_two.make_two_halves(done)
    done = sum_one.make_piece(done, 1)
    sum_one.launch_piece(done)
    sum_two.launch_half(done)
    wgrad_two = sum_two.make_whole(done)
    done = sum_one.make_half(wgrad_two)
    wgrad_one = sum_one.make_whole(done)

    return (
        output.reshape(frames.shape),
        input_gradient.reshape(frames.shape),
        wgrad_one.T,
        gain_grad_one,
        bias_grad_one,
        decay_grad_one,
        wgrad_two.T,
        gain_grad_two,
        bias_grad_two,
        decay_grad_two,
        rms_value,
    )


def solution(mesh):
    return jax.shard_map(
        on_device,
        mesh=mesh,
        in_specs=(
            P(None, "rows", "tm", None),
            P(None, "rows", "tm"),
            P(None, "rows", "tm"),
            P(),
            P(),
            P(),
            P(),
            P(),
            P(),
            P(),
            P(),
            P(None, "rows", "tm", None),
        ),
        out_specs=(
            P(None, "rows", "tm", None),
            P(None, "rows", "tm", None),
            P("tm", None),
            P(),
            P(),
            P(),
            P("tm", None),
            P(),
            P(),
            P(),
            P(),
        ),
        check_vma=False,
    )
```
